32 devices in a mesh: groups: 2 (over y), gy: 4 (over z), gz: 2 (over x), wa: 2 (over core).
Axes of the slice: x: 2, y: 2, z: 4, core: 2. Of those that a mesh axis runs over, the one named last changes fastest.
Arguments:
- velocity: bfloat16 [3, 2048, 8, 1024], P(None, ('groups', 'gy'), ('gz', 'wa')), parts along dimension 1, may hold values from -6 to 6
- line_matrix: bfloat16 [1024, 1024], replicated, may hold values from -1.5 to 1.5
Outputs:
- advanced: bfloat16 [3, 2048, 8, 1024], P(None, ('groups', 'gy'), ('gz', 'wa')), parts along dimension 1
The draws below stay inside these ranges and needn't reach their ends.
There are 2 independent parts, one for each index of `groups`. The reference program is written for one: setup_inputs(seed, part) draws one part's arguments, and reference() takes and returns one part's arrays. A program takes and returns all parts, laid end to end along the dimension named above; an argument that names none is the same for every part. Nothing has to cross between parts.
All inputs are finite; a program needn't handle non-finite values.
Results may differ from the reference program's by a relative error of at most 0.0061.
Values may be sent and summed in bfloat16 or wider, within the bound.
A program may use at most 128 MiB of HBM per device.

```python
import math
import jax
import jax.numpy as jnp
from jax import lax

LINE = 1024
STEPS = 2
NZ = 8


def draw_line_matrix(key, part):
    key = jax.random.fold_in(key, 7)
    noise = jnp.clip(jax.random.normal(key, (LINE, LINE), jnp.float32), -4.0, 4.0)
    row_index = lax.broadcasted_iota(jnp.int32, (LINE, LINE), 0)
    col_index = lax.broadcasted_iota(jnp.int32, (LINE, LINE), 1)
    diagonal = jnp.where(row_index == col_index, 0.75, 0.0)
    return (diagonal + noise * (0.65 / math.sqrt(LINE))).astype(jnp.bfloat16)


def shard_levels(rng, dims, shards, least, top_value):
    level = 1.0
    for axis_at, blocks in shards:
        heights = jax.random.uniform(jax.random.fold_in(jax.random.fold_in(rng, 6), axis_at), (blocks,), jnp.float32, least / len(shards), top_value / len(shards))
        level = level * jnp.repeat(jnp.exp(heights), dims[axis_at] // blocks).reshape((-1,) + (1,) * (len(dims) - 1 - axis_at))
    return level


def scatter_about(key, shape, spread, bound, cuts=(), held_as=jnp.bfloat16):
    factor_of = shard_levels(key, shape, cuts, -0.22, 0.18) if cuts else 1.0
    drawn = jax.random.normal(key, shape, jnp.float32) * spread * factor_of
    return jnp.minimum(jnp.maximum(drawn, -bound), bound).astype(held_as)


def setup_inputs(seed: int = 0, part: int = 0) -> dict:
    streams_of = jax.random.split(jax.random.key(seed), 3)
    own_keys = jax.random.split(jax.random.fold_in(streams_of[2], part), 3)
    return {
        "velocity": scatter_about(own_keys[0], (3, LINE, NZ, LINE), 1.0, 6.0, ((1, 4), (2, 4))),
        "line_matrix": draw_line_matrix(jax.random.fold_in(streams_of[2], 71), part),
    }


courant = 0.2
z_viscous = 0.3


def derivative(values, along):
    return (8.0 * (jnp.roll(values, -1, along) - jnp.roll(values, 1, along)) - (jnp.roll(values, -2, along) - jnp.roll(values, 2, along))) / 12.0


def tendency(current):
    velocity = current.astype(jnp.float32)
    pieces = []
    for component in range(3):
        values = velocity[component]
        advection = velocity[0] * derivative(values, 2) + velocity[1] * derivative(values, 0) + velocity[2] * derivative(values, 1)
        z_diffusion = jnp.roll(values, -1, 1) - 2.0 * values + jnp.roll(values, 1, 1)
        pieces.append((values - courant * advection + z_viscous * z_diffusion).astype(jnp.bfloat16))
    return jnp.stack(pieces)


def along_x(values, matrix):
    return jnp.stack([jnp.einsum('ij,yzj->yzi', matrix, values[component].astype(jnp.float32)).astype(jnp.bfloat16) for component in range(3)])


def along_y(values, matrix):
    return jnp.stack([jnp.einsum('ij,jzx->izx', matrix, values[component].astype(jnp.float32)).astype(jnp.bfloat16) for component in range(3)])


def reference(velocity, line_matrix):
    matrix = line_matrix.astype(jnp.float32)
    current = velocity
    for step_index in range(STEPS):
        forcing = tendency(current)
        if step_index % 2 == 0:
            current = along_y(along_x(forcing, matrix), matrix)
        else:
            current = along_x(along_y(forcing, matrix), matrix)
    return current
```

```python
import jax
import jax.numpy as jnp
from jax import lax
from jax.sharding import PartitionSpec as P

STEPS = 2


courant = 0.2
z_viscous = 0.3


def padded_2(block, sides, width):
    for axis, dim in sides:
        count = lax.axis_size(axis)
        forward = [(i, i + 1) for i in range(count - 1)]
        forward.append((count - 1, 0))
        backward = [(target, source) for source, target in forward]
        low = lax.ppermute(
            lax.slice_in_dim(block, block.shape[dim] - width, None, axis=dim), axis, forward
        )
        high = lax.ppermute(lax.slice_in_dim(block, 0, width, axis=dim), axis, backward)
        block = jnp.concatenate([low, block, high], axis=dim)
    return block


def central(upper_one, lower_one, upper_two, lower_two):
    return (8.0 * (upper_one - lower_one) - (upper_two - lower_two)) / 12.0


def tendency(padded, line_dim, whole_dim):
    planes = padded.shape[2] - 4
    cells = padded.shape[line_dim] - 4

    def crop(line_shift, plane_shift):
        piece = lax.slice_in_dim(padded, line_shift, line_shift + cells, axis=line_dim)
        return lax.slice_in_dim(piece, plane_shift, plane_shift + planes, axis=2).astype(
            jnp.float32
        )

    center = crop(2, 2)
    line_grad = central(crop(3, 2), crop(1, 2), crop(4, 2), crop(0, 2))
    plane_grad = central(crop(2, 3), crop(2, 1), crop(2, 4), crop(2, 0))
    whole_grad = central(
        jnp.roll(center, -1, whole_dim),
        jnp.roll(center, 1, whole_dim),
        jnp.roll(center, -2, whole_dim),
        jnp.roll(center, 2, whole_dim),
    )
    x_grad, y_grad = (whole_grad, line_grad) if line_dim == 1 else (line_grad, whole_grad)
    advection = center[0] * x_grad + center[1] * y_grad + center[2] * plane_grad
    z_diffusion = crop(2, 3) - 2.0 * center + crop(2, 1)
    return (center - courant * advection + z_viscous * z_diffusion).astype(jnp.bfloat16)


def x_solve(values, matrix):
    return jnp.einsum("ij,ayzj->ayzi", matrix, values, preferred_element_type=jnp.float32).astype(
        jnp.bfloat16
    )


def y_solve(values, matrix):
    return jnp.einsum("ij,ajzx->aizx", matrix, values, preferred_element_type=jnp.float32).astype(
        jnp.bfloat16
    )


def body(velocity, line_matrix):
    planes_axis = ("gz", "wa")

    def to_columns(values):
        return lax.all_to_all(values, "gy", split_axis=3, concat_axis=1, tiled=True)

    def to_rows(values):
        return lax.all_to_all(values, "gy", split_axis=1, concat_axis=3, tiled=True)

    padded = padded_2(velocity, ((planes_axis, 2), ("gy", 1)), 2)
    forcing = tendency(padded, 1, 3)
    current = y_solve(to_columns(x_solve(forcing, line_matrix)), line_matrix)
    padded = padded_2(current, ((planes_axis, 2), ("gy", 3)), 2)
    forcing = tendency(padded, 3, 1)
    return x_solve(to_rows(y_solve(forcing, line_matrix)), line_matrix)


def solution(mesh):
    return jax.shard_map(
        body,
        mesh=mesh,
        in_specs=(P(None, ("groups", "gy"), ("gz", "wa"), None), P()),
        out_specs=P(None, ("groups", "gy"), ("gz", "wa"), None),
        check_vma=False,
    )
```

```python
import functools

import jax
import jax.numpy as jnp
from jax import lax
from jax.experimental import pallas as pl
from jax.experimental.pallas import tpu as pltpu
from jax.sharding import PartitionSpec as P

STEPS = 2


courant = 0.2
z_viscous = 0.3


def padded_2(block, sides, width):
    for axis, dim in sides:
        count = lax.axis_size(axis)
        forward = [(i, i + 1) for i in range(count - 1)]
        forward.append((count - 1, 0))
        backward = [(target, source) for source, target in forward]
        low = lax.ppermute(
            lax.slice_in_dim(block, block.shape[dim] - width, None, axis=dim), axis, forward
        )
        high = lax.ppermute(lax.slice_in_dim(block, 0, width, axis=dim), axis, backward)
        block = jnp.concatenate([low, block, high], axis=dim)
    return block


def central(upper_one, lower_one, upper_two, lower_two):
    return (8.0 * (upper_one - lower_one) - (upper_two - lower_two)) / 12.0


def tendency(padded, line_dim, whole_dim):
    planes = padded.shape[2] - 4
    cells = padded.shape[line_dim] - 4

    def crop(line_shift, plane_shift):
        piece = lax.slice_in_dim(padded, line_shift, line_shift + cells, axis=line_dim)
        return lax.slice_in_dim(piece, plane_shift, plane_shift + planes, axis=2).astype(
            jnp.float32
        )

    center = crop(2, 2)
    line_grad = central(crop(3, 2), crop(1, 2), crop(4, 2), crop(0, 2))
    plane_grad = central(crop(2, 3), crop(2, 1), crop(2, 4), crop(2, 0))
    whole_grad = central(
        jnp.roll(center, -1, whole_dim),
        jnp.roll(center, 1, whole_dim),
        jnp.roll(center, -2, whole_dim),
        jnp.roll(center, 2, whole_dim),
    )
    x_grad, y_grad = (whole_grad, line_grad) if line_dim == 1 else (line_grad, whole_grad)
    advection = center[0] * x_grad + center[1] * y_grad + center[2] * plane_grad
    z_diffusion = crop(2, 3) - 2.0 * center + crop(2, 1)
    return (center - courant * advection + z_viscous * z_diffusion).astype(jnp.bfloat16)


def x_solve(values, matrix):
    return jnp.einsum("ij,ayzj->ayzi", matrix, values, preferred_element_type=jnp.float32).astype(
        jnp.bfloat16
    )


def y_solve(values, matrix):
    return jnp.einsum("ij,ajzx->aizx", matrix, values, preferred_element_type=jnp.float32).astype(
        jnp.bfloat16
    )


def body(velocity, line_matrix):
    planes_axis = ("gz", "wa")

    def to_columns(values):
        return lax.all_to_all(values, "gy", split_axis=3, concat_axis=1, tiled=True)

    def to_rows(values):
        return lax.all_to_all(values, "gy", split_axis=1, concat_axis=3, tiled=True)

    padded = padded_2(velocity, ((planes_axis, 2), ("gy", 1)), 2)
    forcing = tendency(padded, 1, 3)
    current = y_solve(to_columns(x_solve(forcing, line_matrix)), line_matrix)
    padded = padded_2(current, ((planes_axis, 2), ("gy", 3)), 2)
    forcing = tendency(padded, 3, 1)
    return x_solve(to_rows(y_solve(forcing, line_matrix)), line_matrix)


CHUNKS = 4
HALO = 16
LANES = 128
MESH = pl.DeviceIdType.MESH


def coefficient(shift):
    near = jnp.where(shift == 1, 8.0, 0.0) + jnp.where(shift == -1, -8.0, 0.0)
    far = jnp.where(shift == 2, -1.0, 0.0) + jnp.where(shift == -2, 1.0, 0.0)
    return near + far


def iota2(shape):
    return lax.broadcasted_iota(jnp.int32, shape, 0), lax.broadcasted_iota(jnp.int32, shape, 1)


def matmul(a, b):
    return jnp.dot(a, b, preferred_element_type=jnp.float32)


def matmul_nt(a, b):
    return lax.dot_general(a, b, (((1,), (1,)), ((), ())), preferred_element_type=jnp.float32)


def steps_kernel(
    sizes,
    v_ref,
    m_ref,
    out_ref,
    ext,
    zh,
    mid,
    col,
    st,
    sib,
    hp,
    hr,
    f2,
    mid2,
    rx,
    band,
    wide,
    frc,
    dxb,
    dyb,
    load_sem,
    y_send,
    y_recv,
    z_send,
    z_recv,
    a_send,
    a_recv,
    s_send,
    s_recv,
    h_send,
    h_recv,
    b_send,
    b_recv,
):
    NQ, NX, NW = sizes
    comps, planes, rows, cells = v_ref.shape
    line = NQ * rows
    depth = NW * planes
    chunk = rows // CHUNKS
    q, X, w = lax.axis_index("gy"), lax.axis_index("gz"), lax.axis_index("wa")
    ring = NX * NW
    zi = X * NW + w
    blocks = NQ * NX
    b = q * NX + X

    def device(dq, dX, dw):
        return {"gy": dq, "gz": dX, "wa": dw}

    def remote(src, dst, send, recv, to):
        return pltpu.make_async_remote_copy(
            src_ref=src, dst_ref=dst, send_sem=send, recv_sem=recv, device_id=to, device_id_type=MESH
        )

    load = pltpu.make_async_copy(v_ref, ext.at[:, :, pl.ds(HALO, rows), :], load_sem)
    load.start()
    barrier = pltpu.get_barrier_semaphore()
    for dq in range(NQ):
        for dX in range(NX):
            for dw in range(NW):
                if dq or dX or dw:
                    to = device(lax.rem(q + dq, NQ), lax.rem(X + dX, NX), lax.rem(w + dw, NW))
                    pl.semaphore_signal(barrier, inc=1, device_id=to, device_id_type=MESH)
    pl.semaphore_wait(barrier, NQ * NX * NW - 1)

    y_copies = []
    for side, (step, start, land) in enumerate(
        ((1, rows - HALO, 0), (NQ - 1, 0, rows + HALO))
    ):
        y_copies.append(
            remote(
                v_ref.at[:, :, pl.ds(start, HALO), :],
                ext.at[:, :, pl.ds(land, HALO), :],
                y_send.at[side],
                y_recv.at[side],
                device(lax.rem(q + step, NQ), X, w),
            )
        )

    def z_copy(side, k):
        other = lax.rem(zi + (1, ring - 1)[side], ring)
        at = pl.ds(pl.multiple_of(k * chunk, chunk), chunk)
        return remote(
            v_ref.at[:, :, at, :],
            zh.at[side, :, :, at, :],
            z_send.at[side, k],
            z_recv.at[side, k],
            device(q, other // NW, lax.rem(other, NW)),
        )

    for copy in y_copies:
        copy.start()
    for k in range(2):
        for side in range(2):
            z_copy(side, k).start()

    i, j = iota2((cells, cells))
    shift = i - j
    shift = jnp.where(shift > cells // 2, shift - cells, shift)
    shift = jnp.where(shift < -(cells // 2), shift + cells, shift)
    band[...] = coefficient(shift).astype(jnp.bfloat16)
    i, j = iota2((chunk, chunk + 2 * HALO))
    local = coefficient(j - HALO - i).astype(jnp.bfloat16)

    load.wait()
    for copy in y_copies:
        copy.wait()

    def a_copy(k, dq, dX):
        to_q, to_X = lax.rem(q + dq, NQ), lax.rem(X + dX, NX)
        lanes = pl.ds(pl.multiple_of((to_q * NX + to_X) * LANES, LANES), LANES)
        src = mid.at[:, :, pl.ds(pl.multiple_of(k * chunk, chunk), chunk), lanes]
        at = pl.ds(pl.multiple_of(q * rows + k * chunk, chunk), chunk)
        dst = col.at[:, pl.ds(w * planes, planes), at, :]
        recv = a_recv.at[k, q * NW + w]
        return (
            lambda: remote(src, dst, a_send.at[k, dq * NX + dX], recv, device(to_q, to_X, X)),
            lambda: pltpu.make_async_copy(src, dst, recv),
        )

    away = [(dq, dx) for dq in (2, 1, 3, 0) if dq < NQ for dx in range(2)]
    away += [(dq, dx) for dq in range(4, NQ) for dx in range(2)]

    def start_pair(pair, own):
        if own is None:
            pair[0]().start()
        else:

            @pl.when(own)
            def _():
                pair[1]().start()

            @pl.when(jnp.logical_not(own))
            def _():
                pair[0]().start()

    def end_send(pair, own):
        if own is None:
            pair[0]().wait_send()
        else:

            @pl.when(jnp.logical_not(own))
            def _():
                pair[0]().wait_send()

    @pl.loop(0, CHUNKS)
    def _(k):
        for side in range(2):
            z_copy(side, k).wait()

        @pl.when(k + 2 < CHUNKS)
        def _():
            for side in range(2):
                z_copy(side, k + 2).start()

        r0 = pl.multiple_of(k * chunk, chunk)
        here = pl.ds(r0, chunk)
        inner = pl.ds(pl.multiple_of(r0 + HALO, HALO), chunk)
        center = ext[:, :, inner, :].reshape(comps * planes * chunk, cells)
        wide[...] = matmul(center, band[...])
        for z in range(planes):
            speed = [ext[c, z, inner, :].astype(jnp.float32) for c in range(comps)]
            for c in range(comps):

                def plane(at):
                    if at < 0:
                        return zh[0, c, at + planes, here, :].astype(jnp.float32)
                    if at >= planes:
                        return zh[1, c, at - planes, here, :].astype(jnp.float32)
                    return ext[c, at, inner, :].astype(jnp.float32)

                y_grad = matmul(local, ext[c, z, pl.ds(r0, chunk + 2 * HALO), :])
                x_grad = wide[pl.ds((c * planes + z) * chunk, chunk), :]
                up, down = plane(z + 1), plane(z - 1)
                z_grad = 8.0 * (up - down) - (plane(z + 2) - plane(z - 2))
                advection = speed[0] * x_grad + speed[1] * y_grad + speed[2] * z_grad
                diffusion = up - 2.0 * speed[c] + down
                frc[pl.ds((c * planes + z) * chunk, chunk), :] = (
                    speed[c] - (courant / 12.0) * advection + z_viscous * diffusion
                ).astype(jnp.bfloat16)
        solved = matmul_nt(frc[...], m_ref[...]).astype(jnp.bfloat16)
        mid[:, :, here, :] = solved.reshape(comps, planes, chunk, cells)
        for dq, dX in away:
            start_pair(a_copy(k, dq, dX), (w == X) if (dq, dX) == (0, 0) else None)

    @pl.loop(0, CHUNKS)
    def _(k):
        for source in range(NQ * NW):
            piece = col.at[:, pl.ds(0, planes), pl.ds(0, chunk), :]
            pltpu.make_async_copy(piece, piece, a_recv.at[k, source]).wait()

    tile = 256

    def sibling(c):
        return remote(
            st.at[c], sib.at[c], s_send.at[c], s_recv.at[c], device(q, X, lax.rem(w + 1, NW))
        )

    @pl.loop(0, comps)
    def _(c):
        right = jnp.concatenate([col[c, z] for z in range(depth)], axis=1)
        for r in range(line // tile):
            at = pl.ds(r * tile, tile)
            solved = matmul(m_ref[at, :], right).astype(jnp.bfloat16)
            for z in range(depth):
                st[c, z, at, :] = solved[:, z * LANES : (z + 1) * LANES]
        sibling(c).start()

    picks = []
    for z in range(comps * depth):
        i, j = iota2((LANES, 2 * LANES))
        right_edge = (i >= LANES - 2) & (j - 4 * z == i - (LANES - 2))
        left_edge = (i < 2) & (j - LANES - 4 * z == i + 2)
        picks.append(jnp.where(right_edge | left_edge, 1.0, 0.0).astype(jnp.bfloat16))
    pick = jnp.concatenate(picks, axis=0)
    for r in range(line // tile):
        at = pl.ds(r * tile, tile)
        left = jnp.concatenate(
            [st[c, z, at, :] for c in range(comps) for z in range(depth)], axis=1
        )
        packed = matmul(left, pick).astype(jnp.bfloat16)
        hp[0, at, :] = packed[:, :LANES]
        hp[1, at, :] = packed[:, LANES:]
    h_copies = []
    for side, step in enumerate((1, blocks - 1)):
        to = lax.rem(b + step, blocks)
        h_copies.append(
            remote(
                hp.at[side],
                hr.at[side],
                h_send.at[side],
                h_recv.at[side],
                device(to // NX, lax.rem(to, NX), w),
            )
        )
    for copy in h_copies:
        copy.start()
    for copy in h_copies:
        copy.wait()
    for c in range(comps):
        sibling(c).wait()
    hp[0] = hr[0] + hr[1]

    def b_copy(c, dq, dw):
        to_q, to_w = lax.rem(q + dq, NQ), lax.rem(w + dw, NW)
        at = pl.ds(pl.multiple_of(to_q * rows, rows), rows)
        src = mid2.at[c, pl.ds(to_w * planes, planes), at, :]
        dst = rx.at[c, :, :, pl.ds(pl.multiple_of(b * LANES, LANES), LANES)]
        recv = b_recv.at[c, b]
        return (
            lambda: remote(src, dst, b_send.at[c, dq * NW + dw], recv, device(to_q, w, to_w)),
            lambda: pltpu.make_async_copy(src, dst, recv),
        )

    @pl.loop(0, comps)
    def _(c):
        right = jnp.concatenate([st[c, z] for z in range(depth)], axis=1)
        for r in range(line // tile):
            at = pl.ds(r * tile, tile)
            dyb[at, :] = matmul(band[at, :], right)
        for z in range(depth):
            i, j = iota2((2 * LANES, LANES))
            k = i - LANES - 4 * (c * depth + z)
            edge = jnp.where(k < 2, k - 2, k - 2 + LANES)
            place = jnp.where(i < LANES, i, edge)
            used = (i < LANES) | ((k >= 0) & (k < 4))
            weights = jnp.where(used, coefficient(place - j), 0.0).astype(jnp.bfloat16)
            both = jnp.concatenate([st[c, z], hp[0]], axis=1)
            dxb[z] = matmul(both, weights)

        @pl.loop(0, line // LANES)
        def _(r):
            at = pl.ds(pl.multiple_of(r * LANES, LANES), LANES)
            own = [st[c, z, at, :].astype(jnp.float32) for z in range(depth)]
            other = [sib[c, z, at, :].astype(jnp.float32) for z in range(depth)]
            ringed = own + other
            for z in range(depth):
                speed = [st[a, z, at, :].astype(jnp.float32) for a in range(comps)]
                up, down = ringed[z + 1], ringed[z - 1]
                z_grad = 8.0 * (up - down) - (ringed[z + 2] - ringed[z - 2])
                advection = (
                    speed[0] * dxb[z, at, :]
                    - speed[1] * dyb[at, z * LANES : (z + 1) * LANES]
                    + speed[2] * z_grad
                )
                diffusion = up - 2.0 * own[z] + down
                f2[c, z, at, :] = (
                    own[z] - (courant / 12.0) * advection + z_viscous * diffusion
                ).astype(jnp.bfloat16)

        forced = jnp.concatenate([f2[c, z] for z in range(depth)], axis=1)
        for r in range(line // tile):
            at = pl.ds(r * tile, tile)
            solved = matmul(m_ref[at, :], forced).astype(jnp.bfloat16)
            for z in range(depth):
                mid2[c, z, at, :] = solved[:, z * LANES : (z + 1) * LANES]
        for dq, dw in away:
            start_pair(b_copy(c, dq, dw), (w == X) if (dq, dw) == (0, 0) else None)

    @pl.loop(0, CHUNKS)
    def _(k):
        for dq, dX in away:
            end_send(a_copy(k, dq, dX), (w == X) if (dq, dX) == (0, 0) else None)

    @pl.loop(0, comps)
    def _(c):
        for source in range(blocks):
            piece = rx.at[c, :, :, pl.ds(0, LANES)]
            pltpu.make_async_copy(piece, piece, b_recv.at[c, source]).wait()
        for z in range(planes):
            out_ref[c, z] = matmul_nt(rx[c, z], m_ref[...]).astype(jnp.bfloat16)
        for dq, dw in away:
            end_send(b_copy(c, dq, dw), (w == X) if (dq, dw) == (0, 0) else None)


def in_one_kernel(sizes, velocity, line_matrix):
    NQ, NX, NW = sizes
    comps, rows, planes, cells = velocity.shape
    line = NQ * rows
    depth = NW * planes
    chunk = rows // CHUNKS
    bf16 = jnp.bfloat16
    columns = pltpu.VMEM((comps, depth, line, LANES), bf16)
    dma = pltpu.SemaphoreType.DMA
    out = pl.pallas_call(
        functools.partial(steps_kernel, sizes),
        out_shape=jax.ShapeDtypeStruct((comps, planes, rows, cells), bf16),
        in_specs=[
            pl.BlockSpec(memory_space=pl.ANY),
            pl.BlockSpec(memory_space=pltpu.VMEM),
        ],
        out_specs=pl.BlockSpec(memory_space=pltpu.VMEM),
        scratch_shapes=[
            pltpu.VMEM((comps, planes, rows + 2 * HALO, cells), bf16),
            pltpu.VMEM((2, comps, planes, rows, cells), bf16),
            pltpu.VMEM((comps, planes, rows, cells), bf16),
            columns,
            columns,
            columns,
            pltpu.VMEM((2, line, LANES), bf16),
            pltpu.VMEM((2, line, LANES), bf16),
            columns,
            columns,
            pltpu.VMEM((comps, planes, rows, cells), bf16),
            pltpu.VMEM((cells, cells), bf16),
            pltpu.VMEM((comps * planes * chunk, cells), jnp.float32),
            pltpu.VMEM((comps * planes * chunk, cells), bf16),
            pltpu.VMEM((depth, line, LANES), jnp.float32),
            pltpu.VMEM((line, depth * LANES), jnp.float32),
            dma,
            dma((2,)),
            dma((2,)),
            dma((2, CHUNKS)),
            dma((2, CHUNKS)),
            dma((CHUNKS, NQ * NX)),
            dma((CHUNKS, NQ * NW)),
            dma((comps,)),
            dma((comps,)),
            dma((2,)),
            dma((2,)),
            dma((comps, NQ * NW)),
            dma((comps, NQ * NX)),
        ],
        compiler_params=pltpu.CompilerParams(
            collective_id=0, has_side_effects=True, vmem_limit_bytes=60 * 1024 * 1024
        ),
    )(jnp.transpose(velocity, (0, 2, 1, 3)), line_matrix)
    return jnp.transpose(out, (0, 2, 1, 3))


def fits(sizes, velocity):
    NQ, NX, NW = sizes
    comps, rows, planes, cells = velocity.shape
    same = NX == 2 and NW == 2 and planes == 2 and cells == NQ * rows
    return same and cells == NQ * NX * LANES and rows % (16 * CHUNKS) == 0 and NQ >= 2


def whole(velocity, line_matrix):
    sizes = tuple(lax.axis_size(axis) for axis in ("gy", "gz", "wa"))
    if fits(sizes, velocity):
        return in_one_kernel(sizes, velocity, line_matrix)
    return body(velocity, line_matrix)


def solution(mesh):
    return jax.shard_map(
        whole,
        mesh=mesh,
        in_specs=(P(None, ("groups", "gy"), ("gz", "wa"), None), P()),
        out_specs=P(None, ("groups", "gy"), ("gz", "wa"), None),
        check_vma=False,
    )
```

```python
import functools

import jax
import jax.numpy as jnp
from jax import lax
from jax.experimental import pallas as pl
from jax.experimental.pallas import tpu as pltpu
from jax.sharding import PartitionSpec as P

STEPS = 2


courant = 0.2
z_viscous = 0.3


def padded_2(block, sides, width):
    for axis, dim in sides:
        count = lax.axis_size(axis)
        forward = [(i, i + 1) for i in range(count - 1)]
        forward.append((count - 1, 0))
        backward = [(target, source) for source, target in forward]
        low = lax.ppermute(
            lax.slice_in_dim(block, block.shape[dim] - width, None, axis=dim), axis, forward
        )
        high = lax.ppermute(lax.slice_in_dim(block, 0, width, axis=dim), axis, backward)
        block = jnp.concatenate([low, block, high], axis=dim)
    return block


def central(upper_one, lower_one, upper_two, lower_two):
    return (8.0 * (upper_one - lower_one) - (upper_two - lower_two)) / 12.0


def tendency(padded, line_dim, whole_dim):
    planes = padded.shape[2] - 4
    cells = padded.shape[line_dim] - 4

    def crop(line_shift, plane_shift):
        piece = lax.slice_in_dim(padded, line_shift, line_shift + cells, axis=line_dim)
        return lax.slice_in_dim(piece, plane_shift, plane_shift + planes, axis=2).astype(
            jnp.float32
        )

    center = crop(2, 2)
    line_grad = central(crop(3, 2), crop(1, 2), crop(4, 2), crop(0, 2))
    plane_grad = central(crop(2, 3), crop(2, 1), crop(2, 4), crop(2, 0))
    whole_grad = central(
        jnp.roll(center, -1, whole_dim),
        jnp.roll(center, 1, whole_dim),
        jnp.roll(center, -2, whole_dim),
        jnp.roll(center, 2, whole_dim),
    )
    x_grad, y_grad = (whole_grad, line_grad) if line_dim == 1 else (line_grad, whole_grad)
    advection = center[0] * x_grad + center[1] * y_grad + center[2] * plane_grad
    z_diffusion = crop(2, 3) - 2.0 * center + crop(2, 1)
    return (center - courant * advection + z_viscous * z_diffusion).astype(jnp.bfloat16)


def x_solve(values, matrix):
    return jnp.einsum("ij,ayzj->ayzi", matrix, values, preferred_element_type=jnp.float32).astype(
        jnp.bfloat16
    )


def y_solve(values, matrix):
    return jnp.einsum("ij,ajzx->aizx", matrix, values, preferred_element_type=jnp.float32).astype(
        jnp.bfloat16
    )


def body(velocity, line_matrix):
    planes_axis = ("gz", "wa")

    def to_columns(values):
        return lax.all_to_all(values, "gy", split_axis=3, concat_axis=1, tiled=True)

    def to_rows(values):
        return lax.all_to_all(values, "gy", split_axis=1, concat_axis=3, tiled=True)

    padded = padded_2(velocity, ((planes_axis, 2), ("gy", 1)), 2)
    forcing = tendency(padded, 1, 3)
    current = y_solve(to_columns(x_solve(forcing, line_matrix)), line_matrix)
    padded = padded_2(current, ((planes_axis, 2), ("gy", 3)), 2)
    forcing = tendency(padded, 3, 1)
    return x_solve(to_rows(y_solve(forcing, line_matrix)), line_matrix)


CHUNKS = 4
HALO = 16
LANES = 128
MESH = pl.DeviceIdType.MESH


def coefficient(shift):
    near = jnp.where(shift == 1, 8.0, 0.0) + jnp.where(shift == -1, -8.0, 0.0)
    far = jnp.where(shift == 2, -1.0, 0.0) + jnp.where(shift == -2, 1.0, 0.0)
    return near + far


def iota2(shape):
    return lax.broadcasted_iota(jnp.int32, shape, 0), lax.broadcasted_iota(jnp.int32, shape, 1)


def matmul(a, b):
    return jnp.dot(a, b, preferred_element_type=jnp.float32)


def matmul_nt(a, b):
    return lax.dot_general(a, b, (((1,), (1,)), ((), ())), preferred_element_type=jnp.float32)


def steps_kernel(
    sizes,
    v_ref,
    m_ref,
    out_ref,
    ext,
    mid,
    col,
    st,
    sib,
    hp,
    hr,
    f2,
    mid2,
    rx,
    band,
    wide,
    frc,
    dxb,
    dyb,
    load_sem,
    y_send,
    y_recv,
    own_send,
    own_recv,
    x_send,
    x_recv,
    f_send,
    f_recv,
    a_send,
    a_recv,
    s_send,
    s_recv,
    h_send,
    h_recv,
    b_send,
    b_recv,
):
    NQ, NX, NW = sizes
    comps, planes, rows, cells = v_ref.shape
    line = NQ * rows
    depth = NW * planes
    half = rows // NX
    chunk = half // CHUNKS
    q, X, w = lax.axis_index("gy"), lax.axis_index("gz"), lax.axis_index("wa")
    ring = depth * NW
    mine = X * depth + w * planes
    theirs = (1 - X) * depth + w * planes
    twin = {"gy": q, "gz": X, "wa": 1 - w}
    blocks = NQ * NX
    b = q * NX + X

    def device(dq, dX, dw):
        return {"gy": dq, "gz": dX, "wa": dw}

    def remote(src, dst, send, recv, to):
        return pltpu.make_async_remote_copy(
            src_ref=src, dst_ref=dst, send_sem=send, recv_sem=recv, device_id=to, device_id_type=MESH
        )

    kept = rows - half + HALO
    own_src = v_ref.at[:, :, pl.ds(pl.multiple_of(X * (half - HALO), HALO), kept), :]
    own_dst = ext.at[:, pl.ds(mine, planes), pl.ds(pl.multiple_of((1 - X) * HALO, HALO), kept), :]
    load = pltpu.make_async_copy(own_src, own_dst, load_sem)
    load.start()
    barrier = pltpu.get_barrier_semaphore()
    for dq in range(NQ):
        for dX in range(NX):
            for dw in range(NW):
                if dq or dX or dw:
                    to = device(lax.rem(q + dq, NQ), lax.rem(X + dX, NX), lax.rem(w + dw, NW))
                    pl.semaphore_signal(barrier, inc=1, device_id=to, device_id_type=MESH)
    pl.semaphore_wait(barrier, NQ * NX * NW - 1)

    y_copies = []
    for side, (step, start, land) in enumerate(
        ((1, rows - HALO, 0), (NQ - 1, 0, half + HALO))
    ):
        y_copies.append(
            remote(
                v_ref.at[:, :, pl.ds(start, HALO), :],
                ext.at[:, pl.ds(mine, planes), pl.ds(land, HALO), :],
                y_send.at[side],
                y_recv.at[w],
                device(lax.rem(q + step, NQ), side, X),
            )
        )
    to_twin = remote(own_src, own_dst, own_send, own_recv, twin)

    def part(half_at, k):
        if isinstance(k, int) and k == 0:
            return pl.multiple_of(HALO + half_at * (half - HALO), HALO), HALO
        down = half - chunk * k
        up = 2 * HALO + chunk * (k - 1)
        return pl.multiple_of(up + half_at * (down - up), HALO), chunk

    def x_copy(k):
        at, count = part(1 - X, k)
        start = pl.multiple_of(at - HALO + (1 - X) * half, HALO)
        return remote(
            v_ref.at[:, :, pl.ds(start, count), :],
            ext.at[:, pl.ds(mine, planes), pl.ds(at, count), :],
            x_send.at[k],
            x_recv.at[k],
            device(q, 1 - X, w),
        )

    def forward(k):
        at, count = part(X, k)
        piece = ext.at[:, pl.ds(theirs, planes), pl.ds(at, count), :]
        return remote(piece, piece, f_send.at[k], f_recv.at[k], twin)

    for k in range(2):
        x_copy(k).start()
    to_twin.start()
    for copy in y_copies:
        copy.start()
    x_copy(2).start()

    i, j = iota2((cells, cells))
    shift = i - j
    shift = jnp.where(shift > cells // 2, shift - cells, shift)
    shift = jnp.where(shift < -(cells // 2), shift + cells, shift)
    band[...] = coefficient(shift).astype(jnp.bfloat16)
    i, j = iota2((chunk, chunk + 2 * HALO))
    local = coefficient(j - HALO - i).astype(jnp.bfloat16)

    load.wait()
    to_twin.wait()
    for side, copy in enumerate(y_copies):
        copy.wait_send()
        piece = ext.at[:, pl.ds(0, planes), pl.ds(0, HALO), :]
        pltpu.make_async_copy(piece, piece, y_recv.at[side]).wait()
    x_copy(0).wait()
    forward(0).start()
    forward(0).wait()

    def a_copy(k, dq, dX):
        to_q, to_X = lax.rem(q + dq, NQ), lax.rem(X + dX, NX)
        lanes = pl.ds(pl.multiple_of((to_q * NX + to_X) * LANES, LANES), LANES)
        src = mid.at[:, :, pl.ds(pl.multiple_of(k * chunk, chunk), chunk), lanes]
        at = pl.ds(pl.multiple_of(q * rows + X * half + k * chunk, chunk), chunk)
        dst = col.at[:, :, at, :]
        recv = a_recv.at[k, q * NX + X]
        if (dq, dX) == (0, 0):
            return pltpu.make_async_copy(src, dst, recv)
        return remote(src, dst, a_send.at[k, dq * NX + dX], recv, device(to_q, to_X, w))

    away = [(dq, dx) for dq in (2, 1, 3, 0) if dq < NQ for dx in range(2)]
    away += [(dq, dx) for dq in range(4, NQ) for dx in range(2)]

    def start_pair(pair, own):
        if own is None:
            pair[0]().start()
        else:

            @pl.when(own)
            def _():
                pair[1]().start()

            @pl.when(jnp.logical_not(own))
            def _():
                pair[0]().start()

    def end_send(pair, own):
        if own is None:
            pair[0]().wait_send()
        else:

            @pl.when(jnp.logical_not(own))
            def _():
                pair[0]().wait_send()

    @pl.loop(0, CHUNKS)
    def _(n):
        x_copy(n + 1).wait()
        forward(n + 1).start()

        @pl.when(n + 2 < CHUNKS)
        def _():
            x_copy(n + 3).start()

        forward(n + 1).wait()
        k = n + X * (CHUNKS - 1 - 2 * n)
        r0 = pl.multiple_of(k * chunk, chunk)
        here = pl.ds(r0, chunk)
        inner = pl.ds(pl.multiple_of(r0 + HALO, HALO), chunk)
        center = ext[:, pl.ds(w * depth, depth), inner, :].reshape(comps * depth * chunk, cells)
        wide[...] = matmul(center, band[...])
        for z in range(depth):
            at = w * depth + z
            speed = [ext[c, at, inner, :].astype(jnp.float32) for c in range(comps)]
            for c in range(comps):

                def plane(shift):
                    return ext[c, lax.rem(at + shift + ring, ring), inner, :].astype(jnp.float32)

                y_grad = matmul(local, ext[c, at, pl.ds(r0, chunk + 2 * HALO), :])
                lines = pl.ds((c * depth + z) * chunk, chunk)
                x_grad = wide[lines, :]
                up, down = plane(1), plane(-1)
                z_grad = 8.0 * (up - down) - (plane(2) - plane(-2))
                advection = speed[0] * x_grad + speed[1] * y_grad + speed[2] * z_grad
                diffusion = up - 2.0 * speed[c] + down
                frc[lines, :] = (
                    speed[c] - (courant / 12.0) * advection + z_viscous * diffusion
                ).astype(jnp.bfloat16)
        solved = matmul_nt(frc[...], m_ref[...]).astype(jnp.bfloat16)
        mid[:, :, here, :] = solved.reshape(comps, depth, chunk, cells)
        for dq, dX in away:
            a_copy(k, dq, dX).start()

    @pl.loop(0, CHUNKS)
    def _(k):
        for source in range(NQ * NX):
            piece = col.at[:, :, pl.ds(0, chunk), :]
            pltpu.make_async_copy(piece, piece, a_recv.at[k, source]).wait()

    tile = 256

    def sibling(c):
        return remote(
            st.at[c], sib.at[c], s_send.at[c], s_recv.at[c], device(q, X, lax.rem(w + 1, NW))
        )

    @pl.loop(0, comps)
    def _(c):
        right = jnp.concatenate([col[c, z] for z in range(depth)], axis=1)
        for r in range(line // tile):
            at = pl.ds(r * tile, tile)
            solved = matmul(m_ref[at, :], right).astype(jnp.bfloat16)
            for z in range(depth):
                st[c, z, at, :] = solved[:, z * LANES : (z + 1) * LANES]
        sibling(c).start()

    picks = []
    for z in range(comps * depth):
        i, j = iota2((LANES, 2 * LANES))
        right_edge = (i >= LANES - 2) & (j - 4 * z == i - (LANES - 2))
        left_edge = (i < 2) & (j - LANES - 4 * z == i + 2)
        picks.append(jnp.where(right_edge | left_edge, 1.0, 0.0).astype(jnp.bfloat16))
    pick = jnp.concatenate(picks, axis=0)
    for r in range(line // tile):
        at = pl.ds(r * tile, tile)
        left = jnp.concatenate(
            [st[c, z, at, :] for c in range(comps) for z in range(depth)], axis=1
        )
        packed = matmul(left, pick).astype(jnp.bfloat16)
        hp[0, at, :] = packed[:, :LANES]
        hp[1, at, :] = packed[:, LANES:]
    h_copies = []
    for side, step in enumerate((1, blocks - 1)):
        to = lax.rem(b + step, blocks)
        h_copies.append(
            remote(
                hp.at[side],
                hr.at[side],
                h_send.at[side],
                h_recv.at[side],
                device(to // NX, lax.rem(to, NX), w),
            )
        )
    for copy in h_copies:
        copy.start()
    for copy in h_copies:
        copy.wait()
    for c in range(comps):
        sibling(c).wait()
    hp[0] = hr[0] + hr[1]

    def b_copy(c, dq, dw):
        to_q, to_w = lax.rem(q + dq, NQ), lax.rem(w + dw, NW)
        at = pl.ds(pl.multiple_of(to_q * rows, rows), rows)
        src = mid2.at[c, pl.ds(to_w * planes, planes), at, :]
        dst = rx.at[c, :, :, pl.ds(pl.multiple_of(b * LANES, LANES), LANES)]
        recv = b_recv.at[c, b]
        return (
            lambda: remote(src, dst, b_send.at[c, dq * NW + dw], recv, device(to_q, w, to_w)),
            lambda: pltpu.make_async_copy(src, dst, recv),
        )

    @pl.loop(0, comps)
    def _(c):
        right = jnp.concatenate([st[c, z] for z in range(depth)], axis=1)
        for r in range(line // tile):
            at = pl.ds(r * tile, tile)
            dyb[at, :] = matmul(band[at, :], right)
        for z in range(depth):
            i, j = iota2((2 * LANES, LANES))
            k = i - LANES - 4 * (c * depth + z)
            edge = jnp.where(k < 2, k - 2, k - 2 + LANES)
            place = jnp.where(i < LANES, i, edge)
            used = (i < LANES) | ((k >= 0) & (k < 4))
            weights = jnp.where(used, coefficient(place - j), 0.0).astype(jnp.bfloat16)
            both = jnp.concatenate([st[c, z], hp[0]], axis=1)
            dxb[z] = matmul(both, weights)

        @pl.loop(0, line // LANES)
        def _(r):
            at = pl.ds(pl.multiple_of(r * LANES, LANES), LANES)
            own = [st[c, z, at, :].astype(jnp.float32) for z in range(depth)]
            other = [sib[c, z, at, :].astype(jnp.float32) for z in range(depth)]
            ringed = own + other
            for z in range(depth):
                speed = [st[a, z, at, :].astype(jnp.float32) for a in range(comps)]
                up, down = ringed[z + 1], ringed[z - 1]
                z_grad = 8.0 * (up - down) - (ringed[z + 2] - ringed[z - 2])
                advection = (
                    speed[0] * dxb[z, at, :]
                    - speed[1] * dyb[at, z * LANES : (z + 1) * LANES]
                    + speed[2] * z_grad
                )
                diffusion = up - 2.0 * own[z] + down
                f2[c, z, at, :] = (
                    own[z] - (courant / 12.0) * advection + z_viscous * diffusion
                ).astype(jnp.bfloat16)

        forced = jnp.concatenate([f2[c, z] for z in range(depth)], axis=1)
        for r in range(line // tile):
            at = pl.ds(r * tile, tile)
            solved = matmul(m_ref[at, :], forced).astype(jnp.bfloat16)
            for z in range(depth):
                mid2[c, z, at, :] = solved[:, z * LANES : (z + 1) * LANES]
        for dq, dw in away:
            start_pair(b_copy(c, dq, dw), (w == X) if (dq, dw) == (0, 0) else None)

    @pl.loop(0, CHUNKS)
    def _(k):
        for dq, dX in away:
            if (dq, dX) != (0, 0):
                a_copy(k, dq, dX).wait_send()

    @pl.loop(0, comps)
    def _(c):
        for source in range(blocks):
            piece = rx.at[c, :, :, pl.ds(0, LANES)]
            pltpu.make_async_copy(piece, piece, b_recv.at[c, source]).wait()
        for z in range(planes):
            out_ref[c, z] = matmul_nt(rx[c, z], m_ref[...]).astype(jnp.bfloat16)
        for dq, dw in away:
            end_send(b_copy(c, dq, dw), (w == X) if (dq, dw) == (0, 0) else None)


def in_one_kernel(sizes, velocity, line_matrix):
    NQ, NX, NW = sizes
    comps, rows, planes, cells = velocity.shape
    line = NQ * rows
    depth = NW * planes
    half = rows // NX
    chunk = half // CHUNKS
    bf16 = jnp.bfloat16
    columns = pltpu.VMEM((comps, depth, line, LANES), bf16)
    dma = pltpu.SemaphoreType.DMA
    out = pl.pallas_call(
        functools.partial(steps_kernel, sizes),
        out_shape=jax.ShapeDtypeStruct((comps, planes, rows, cells), bf16),
        in_specs=[
            pl.BlockSpec(memory_space=pl.ANY),
            pl.BlockSpec(memory_space=pltpu.VMEM),
        ],
        out_specs=pl.BlockSpec(memory_space=pltpu.VMEM),
        scratch_shapes=[
            pltpu.VMEM((comps, NX * depth, half + 2 * HALO, cells), bf16),
            pltpu.VMEM((comps, depth, half, cells), bf16),
            columns,
            columns,
            columns,
            pltpu.VMEM((2, line, LANES), bf16),
            pltpu.VMEM((2, line, LANES), bf16),
            columns,
            columns,
            pltpu.VMEM((comps, planes, rows, cells), bf16),
            pltpu.VMEM((cells, cells), bf16),
            pltpu.VMEM((comps * depth * chunk, cells), jnp.float32),
            pltpu.VMEM((comps * depth * chunk, cells), bf16),
            pltpu.VMEM((depth, line, LANES), jnp.float32),
            pltpu.VMEM((line, depth * LANES), jnp.float32),
            dma,
            dma((2,)),
            dma((2,)),
            dma,
            dma,
            dma((CHUNKS + 1,)),
            dma((CHUNKS + 1,)),
            dma((CHUNKS + 1,)),
            dma((CHUNKS + 1,)),
            dma((CHUNKS, NQ * NX)),
            dma((CHUNKS, NQ * NX)),
            dma((comps,)),
            dma((comps,)),
            dma((2,)),
            dma((2,)),
            dma((comps, NQ * NW)),
            dma((comps, NQ * NX)),
        ],
        compiler_params=pltpu.CompilerParams(
            collective_id=0, has_side_effects=True, vmem_limit_bytes=60 * 1024 * 1024
        ),
    )(jnp.transpose(velocity, (0, 2, 1, 3)), line_matrix)
    return jnp.transpose(out, (0, 2, 1, 3))


def fits(sizes, velocity):
    NQ, NX, NW = sizes
    comps, rows, planes, cells = velocity.shape
    same = NX == 2 and NW == 2 and planes == 2 and cells == NQ * rows
    return same and cells == NQ * NX * LANES and rows % (32 * NX * CHUNKS) == 0 and NQ >= 2


def whole(velocity, line_matrix):
    sizes = tuple(lax.axis_size(axis) for axis in ("gy", "gz", "wa"))
    if fits(sizes, velocity):
        return in_one_kernel(sizes, velocity, line_matrix)
    return body(velocity, line_matrix)


def solution(mesh):
    return jax.shard_map(
        whole,
        mesh=mesh,
        in_specs=(P(None, ("groups", "gy"), ("gz", "wa"), None), P()),
        out_specs=P(None, ("groups", "gy"), ("gz", "wa"), None),
        check_vma=False,
    )
```
